32 devices in a mesh: groups: 2 (over y), tensor: 4 (over z), rows: 2 (over x), role: 2 (over core).
Axes of the slice: x: 2, y: 2, z: 4, core: 2. Of those that a mesh axis runs over, the one named last changes fastest.
Arguments:
- residual: bfloat16 [64, 8192], P(('groups', 'tensor'), ('rows', 'role')), parts along dimension 0, may hold values from -6 to 6
- attn_gain: float32 [8192], P(('rows', 'role')), may hold values from 0.1 to 1.9
- attn_proj: bfloat16 [3, 8192, 8192], P(None, ('rows', 'role'), 'tensor'), may hold values from -0.0625 to 0.0625
- cache_keys: bfloat16 [64, 32, 8192], P(('groups', 'rows', 'role'), None, 'tensor'), parts along dimension 0, may hold values from -600 to 600
- cache_values: bfloat16 [64, 32, 8192], P(('groups', 'rows', 'role'), None, 'tensor'), parts along dimension 0, may hold values from -6 to 6
- lengths: int32 [64], P(('groups', 'rows', 'role')), parts along dimension 0, may hold values from 1 to 32
- placement: int32 [64], P('groups'), parts along dimension 0, may hold values from 0 to 31, each once
- out_proj: bfloat16 [8192, 8192], P('tensor', ('rows', 'role')), may hold values from -0.0625 to 0.0625
- mix_gain: float32 [8192], P(('rows', 'role')), may hold values from 0.1 to 1.9
- mix_proj: bfloat16 [3, 8192, 8192], P(None, ('rows', 'role'), 'tensor'), may hold values from -0.0625 to 0.0625
- outer_taps: float32 [3, 3, 8192], P(None, None, 'tensor'), may hold values from -1 to 1
- outer_state: bfloat16 [2, 3, 64, 8192], P(None, None, ('groups', 'rows', 'role'), 'tensor'), parts along dimension 2, may hold values from -6 to 6
- inner_taps: float32 [3, 8192], P(None, 'tensor'), may hold values from -1 to 1
- inner_state: bfloat16 [2, 64, 8192], P(None, ('groups', 'rows', 'role'), 'tensor'), parts along dimension 1, may hold values from -6 to 6
Outputs:
- attended: bfloat16 [64, 8192], P(('groups', 'tensor'), ('rows', 'role')), parts along dimension 0
- gated: bfloat16 [64, 8192], P(('groups', 'rows', 'role'), 'tensor'), parts along dimension 0
The draws below stay inside these ranges and needn't reach their ends.
There are 2 independent parts, one for each index of `groups`. The reference program is written for one: setup_inputs(seed, part) draws one part's arguments, and reference() takes and returns one part's arrays. A program takes and returns all parts, laid end to end along the dimension named above; an argument that names none is the same for every part. Nothing has to cross between parts.
Inputs may be any that keep to these rules, and one draw needn't show every extreme that they name: Cache slot s holds lengths[s] cached positions, the first of its 32. `placement`: each row has its own cache slot.
All inputs are finite; a program needn't handle non-finite values.
Results may differ from the reference program's by a relative error of at most 0.017.
Values may be sent and summed in bfloat16 or wider, within the bound.
A program may use at most 128 MiB of HBM per device.

```python
import math
import jax
import jax.numpy as jnp
from jax import lax

D = 8192
HEADS = 64
HEAD_DIM = 128
CTX = 32
BATCH = 32


def draw_cache_keys(key, part):
    base = jnp.clip(jax.random.normal(jax.random.fold_in(key, 11), (BATCH, CTX, D), jnp.float32), -4.0, 4.0)
    return base.astype(jnp.bfloat16)


def set_ends(drawn, rng, smallest, largest):
    spot = [jax.random.randint(jax.random.fold_in(rng, axis), (), 0, length) for axis, length in enumerate(drawn.shape)]
    longest = drawn.shape.index(max(drawn.shape))
    next_to = spot[:longest] + [(spot[longest] + 1) % drawn.shape[longest]] + spot[longest + 1:]
    return drawn.at[tuple(spot)].set(smallest).at[tuple(next_to)].set(largest)


def shard_levels(stream_key, shape, pieces, low, largest):
    factor_of = 1.0
    for axis_at, blocks in pieces:
        heights = jax.random.uniform(jax.random.fold_in(jax.random.fold_in(stream_key, 6), axis_at), (blocks,), jnp.float32, low / len(pieces), largest / len(pieces))
        factor_of = factor_of * jnp.repeat(jnp.exp(heights), shape[axis_at] // blocks).reshape((-1,) + (1,) * (len(shape) - 1 - axis_at))
    return factor_of


def scatter_about(stream_key, extent, deviation, reach, pieces=(), held_as=jnp.bfloat16):
    entries = deviation * jax.random.normal(stream_key, extent, jnp.float32)
    if pieces:
        entries = entries * shard_levels(stream_key, extent, pieces, -0.22, 0.18)
    return jnp.clip(entries, -reach, reach).astype(held_as)


def setup_inputs(seed: int = 0, part: int = 0) -> dict:
    splits = jax.random.split(jax.random.key(seed), 15)
    part_keys = jax.random.split(jax.random.fold_in(splits[14], part), 15)
    return {
        "residual": scatter_about(part_keys[0], (BATCH, D), 1.0, 6.0, ((0, 4), (1, 4))),
        "attn_gain": jnp.clip(1.0 + 0.18 * jax.random.normal(splits[1], (D,), jnp.float32), 0.1, 1.9),
        "attn_proj": scatter_about(splits[2], (3, D, D), D ** -0.5, 0.0625, ((1, 4), (2, 4))),
        "cache_keys": draw_cache_keys(jax.random.fold_in(jax.random.fold_in(splits[14], part), 71), part),
        "cache_values": scatter_about(part_keys[4], (BATCH, CTX, D), 1.0, 6.0, ((0, 4), (2, 4))),
        "lengths": set_ends(jax.random.randint(part_keys[5], (BATCH,), 1, CTX + 1), jax.random.fold_in(part_keys[5], 1), 1, CTX).astype(jnp.int32),
        "placement": jax.random.permutation(part_keys[6], BATCH).astype(jnp.int32),
        "out_proj": scatter_about(splits[7], (D, D), D ** -0.5, 0.0625, ((0, 4), (1, 4))),
        "mix_gain": jnp.clip(1.0 + 0.18 * jax.random.normal(splits[8], (D,), jnp.float32), 0.1, 1.9),
        "mix_proj": scatter_about(splits[9], (3, D, D), D ** -0.5, 0.0625, ((1, 4), (2, 4))),
        "outer_taps": jnp.clip(jax.random.uniform(splits[10], (3, 3, D), jnp.float32, -1.0, 1.0) * shard_levels(splits[10], (3, 3, D), ((2, 4),), -0.4, 0.0), -1.0, 1.0),
        "outer_state": scatter_about(part_keys[11], (2, 3, BATCH, D), 1.0, 6.0, ((2, 4), (3, 4))),
        "inner_taps": jnp.clip(jax.random.uniform(splits[12], (3, D), jnp.float32, -1.0, 1.0) * shard_levels(splits[12], (3, D), ((1, 4),), -0.4, 0.0), -1.0, 1.0),
        "inner_state": scatter_about(part_keys[13], (2, BATCH, D), 1.0, 6.0, ((1, 4), (2, 4))),
    }


def reference(residual, attn_gain, attn_proj, cache_keys, cache_values, lengths, placement, out_proj, mix_gain, mix_proj, outer_taps, outer_state, inner_taps, inner_state):
    widened = residual.astype(jnp.float32)
    normed = (widened * lax.rsqrt(lax.optimization_barrier(jnp.mean(widened * widened, axis=1, keepdims=True)) + 1e-05) * attn_gain).astype(jnp.bfloat16)
    triple = jnp.stack([jnp.dot(normed, attn_proj[j], preferred_element_type=jnp.float32) for j in range(3)]).astype(jnp.bfloat16)
    inverse = jnp.zeros((BATCH,), jnp.int32).at[placement].set(jnp.arange(BATCH, dtype=jnp.int32))
    ordered = jnp.take(triple, inverse, axis=1)
    query = ordered[0].astype(jnp.float32).reshape(BATCH, HEADS, HEAD_DIM)
    fresh_key = ordered[1].astype(jnp.float32).reshape(BATCH, HEADS, HEAD_DIM)
    fresh_value = ordered[2].astype(jnp.float32).reshape(BATCH, HEADS, HEAD_DIM)
    keys_wide = cache_keys.astype(jnp.float32).reshape(BATCH, CTX, HEADS, HEAD_DIM)
    values_wide = cache_values.astype(jnp.float32).reshape(BATCH, CTX, HEADS, HEAD_DIM)
    scale = 1.0 / math.sqrt(HEAD_DIM)
    scores = jnp.einsum('shd,sphd->shp', query, keys_wide) * scale
    own_score = lax.optimization_barrier(jnp.sum(query * fresh_key, axis=2)) * scale
    live = jnp.arange(CTX, dtype=jnp.int32)[None, None, :] < lengths[:, None, None]
    top_score = jnp.maximum(lax.optimization_barrier(jnp.max(jnp.where(live, scores, -jnp.inf), axis=2)), own_score)
    probs = jnp.where(live, jnp.exp(scores - top_score[:, :, None]), 0.0)
    self_prob = jnp.exp(own_score - top_score)
    total = lax.optimization_barrier(jnp.sum(probs, axis=2)) + self_prob
    weights = (probs / total[:, :, None]).astype(jnp.bfloat16).astype(jnp.float32)
    self_weight = (self_prob / total).astype(jnp.bfloat16).astype(jnp.float32)
    mixed = jnp.einsum('shp,sphd->shd', weights, values_wide) + self_weight[:, :, None] * fresh_value
    slot_out = mixed.reshape(BATCH, D).astype(jnp.bfloat16)
    heads_out = jnp.take(slot_out, placement, axis=0)
    attended = (widened + jnp.dot(heads_out, out_proj, preferred_element_type=jnp.float32)).astype(jnp.bfloat16)
    attended_wide = attended.astype(jnp.float32)
    mix_normed = (attended_wide * lax.rsqrt(lax.optimization_barrier(jnp.mean(attended_wide * attended_wide, axis=1, keepdims=True)) + 1e-05) * mix_gain).astype(jnp.bfloat16)
    branches = jnp.stack([jnp.dot(mix_normed, mix_proj[j], preferred_element_type=jnp.float32) for j in range(3)])
    conv = outer_taps[0][:, None, :] * branches + outer_taps[1][:, None, :] * outer_state[0].astype(jnp.float32) + outer_taps[2][:, None, :] * outer_state[1].astype(jnp.float32)
    product = conv[0] * conv[2]
    filtered = inner_taps[0] * product + inner_taps[1] * inner_state[0].astype(jnp.float32) + inner_taps[2] * inner_state[1].astype(jnp.float32)
    gated = (conv[1] * filtered).astype(jnp.bfloat16)
    return (attended, gated)
```

```python
import functools
import math

import jax
import jax.numpy as jnp
from jax import lax
from jax.experimental import pallas as pl
from jax.experimental.pallas import tpu as pltpu
from jax.sharding import PartitionSpec as P

HEAD_DIM = 128
LANES = 128
COLUMNS = 256
MESH = pl.DeviceIdType.MESH
F32 = jnp.float32
BF16 = jnp.bfloat16


def quotient(a, n):
    if n & (n - 1) == 0:
        return lax.shift_right_logical(a, jnp.int32(n.bit_length() - 1))
    return lax.div(a, jnp.int32(n))


def iota(shape, axis):
    return lax.broadcasted_iota(jnp.int32, shape, axis)


def flag(mask):
    return jnp.where(mask, 1.0, 0.0).astype(BF16)


def matmul(a, b):
    return jnp.dot(a, b, preferred_element_type=F32)


def matmul_nt(a, b):
    return lax.dot_general(a, b, (((1,), (1,)), ((), ())), preferred_element_type=F32)


def matmul_tn(a, b):
    return lax.dot_general(a, b, (((0,), (0,)), ((), ())), preferred_element_type=F32)


def kernel(
    nt,
    nr,
    nc,
    x_hbm,
    again_hbm,
    aproj_hbm,
    keys_hbm,
    vals_hbm,
    lens_ref,
    place_row_ref,
    oproj_hbm,
    mgain_hbm,
    mproj_hbm,
    otaps_hbm,
    ostate_hbm,
    itaps_hbm,
    istate_hbm,
    att_ref,
    gated_ref,
    xv,
    gainv,
    mgainv,
    wa,
    wo,
    wm,
    kv,
    vv,
    otv,
    osv,
    itv,
    isv,
    sq_send,
    sq_recv,
    nbuf,
    tbuf,
    rbuf,
    hbuf,
    obuf,
    robuf,
    abuf,
    msq_send,
    msq_recv,
    mbuf,
    rmbuf,
    lsem,
    wsem,
    sq_sems,
    n_sems,
    t_sems,
    h_sems,
    o_sems,
    a_sems,
    msq_sems,
    m_sems,
):
    ng = nr * nc
    me_t = lax.axis_index("tensor")
    me_g = lax.axis_index("rows") * nc + lax.axis_index("role")
    xb, feat = xv.shape
    width = wa.shape[2]
    slots, ctx = kv.shape[0], kv.shape[1]
    heads = width // HEAD_DIM
    batch = nt * xb
    total_feat = feat * ng

    def t_peer(k):
        return lax.rem(me_t + k, nt)

    def g_peer(k):
        return lax.rem(me_g + k, ng)

    def t_id(k):
        return {"tensor": t_peer(k)}

    def g_id(k):
        p = g_peer(k)
        return {"rows": lax.div(p, nc), "role": lax.rem(p, nc)}

    def remote(src, dst, sems, at, device):
        return pltpu.make_async_remote_copy(
            src_ref=src,
            dst_ref=dst,
            send_sem=sems.at[(0,) + at],
            recv_sem=sems.at[(1,) + at],
            device_id=device,
            device_id_type=MESH,
        )

    barrier = pltpu.get_barrier_semaphore()
    for k in range(1, nt):
        pl.semaphore_signal(barrier, inc=1, device_id=t_id(k), device_id_type=MESH)
    for k in range(1, ng):
        pl.semaphore_signal(barrier, inc=1, device_id=g_id(k), device_id_type=MESH)

    small = [
        pltpu.make_async_copy(s, d, lsem.at[i])
        for i, (s, d) in enumerate(
            [
                (x_hbm, xv),
                (again_hbm, gainv),
                (mgain_hbm, mgainv),
                (keys_hbm, kv),
                (vals_hbm, vv),
                (otaps_hbm, otv),
                (ostate_hbm, osv),
                (itaps_hbm, itv),
                (istate_hbm, isv),
            ]
        )
    ]
    a_copies = [pltpu.make_async_copy(aproj_hbm.at[j], wa.at[j], wsem.at[j]) for j in range(3)]
    o_copy = pltpu.make_async_copy(oproj_hbm, wo, wsem.at[3])
    m_homes = [wm, wa.at[0], wa.at[1]]
    m_copies = [
        pltpu.make_async_copy(mproj_hbm.at[j], m_homes[j], wsem.at[4 + j]) for j in range(3)
    ]
    small[0].start()
    small[1].start()
    for c in a_copies:
        c.start()
    for c in small[2:]:
        c.start()
    o_copy.start()
    m_copies[0].start()

    small[0].wait()
    small[1].wait()
    x = xv[...].astype(F32)
    sq_send[...] = jnp.broadcast_to(jnp.sum(x * x, axis=1, keepdims=True), sq_send.shape)
    pl.semaphore_wait(barrier, (nt - 1) + (ng - 1))
    pending = []
    copies = [remote(sq_send, sq_recv.at[k - 1], sq_sems, (k - 1,), g_id(k)) for k in range(1, ng)]
    for c in copies:
        c.start()
    pending += copies
    for c in copies:
        c.wait_recv()
    squares = sq_send[...]
    for k in range(ng - 1):
        squares = squares + sq_recv[k]
    scale_rows = lax.rsqrt(squares[:, :1] / total_feat + 1e-05)
    nbuf[me_t] = (x * scale_rows * gainv[...]).astype(BF16)
    copies = [
        remote(nbuf.at[me_t], nbuf.at[me_t], n_sems, (k - 1,), t_id(k)) for k in range(1, nt)
    ]
    for c in copies:
        c.start()
    pending += copies

    place_row = place_row_ref[...]
    to_slots = flag(place_row == iota((batch, batch), 0))
    for c in copies:
        c.wait_recv()
    normed = nbuf[...].astype(F32).reshape(batch, feat).astype(BF16)
    normed = matmul(to_slots, normed).astype(BF16)

    cols = min(COLUMNS, width)
    t_copies = []
    for j in range(3):
        a_copies[j].wait()

        def attn_step(c, carry, j=j):
            at = pl.ds(pl.multiple_of(c * cols, cols), cols)
            term = matmul(normed, wa[j, :, at])
            for g in range(ng):
                tbuf[g, j, :, at] = term[g * slots : (g + 1) * slots]
            return carry

        lax.fori_loop(0, width // cols, attn_step, 0)
        if j < 2:
            m_copies[1 + j].start()
        step = [
            remote(tbuf.at[g_peer(k), j], rbuf.at[k - 1, j], t_sems, (k - 1, j), g_id(k))
            for k in range(1, ng)
        ]
        for c in step:
            c.start()
        t_copies.append(step)
        pending += step

    rows = slots * heads
    expand_mask = quotient(iota((rows, slots), 0), heads) == iota((rows, slots), 1)
    expand = flag(expand_mask)
    collapse = flag(quotient(iota((slots, rows), 1), heads) == iota((slots, rows), 0))
    row_at = iota((rows, width), 0)
    head_mask = quotient(iota((rows, width), 1), HEAD_DIM) == row_at - heads * quotient(row_at, heads)
    row_at = iota((rows, slots * ctx), 0)
    col_at = iota((rows, slots * ctx), 1)
    col_slot = quotient(col_at, ctx)
    row_length = jnp.sum(
        jnp.where(expand_mask, lens_ref[...].astype(F32), 0.0), axis=1, keepdims=True
    )
    live = (quotient(row_at, heads) == col_slot) & (
        (col_at - ctx * col_slot).astype(F32) < row_length
    )

    triple = []
    small[3].wait()
    small[4].wait()
    for j in range(3):
        for c in t_copies[j]:
            c.wait_recv()
        total = tbuf[me_g, j]
        for k in range(ng - 1):
            total = total + rbuf[k, j]
        triple.append(total.astype(BF16))
    query, fresh_key, fresh_value = triple

    scale = 1.0 / math.sqrt(HEAD_DIM)
    spread = jnp.where(head_mask, matmul(expand, query), 0.0).astype(BF16)
    scores = matmul_nt(spread, kv[...].reshape(slots * ctx, width)) * scale
    own = (
        jnp.sum(
            jnp.where(expand_mask, matmul_nt(spread, fresh_key), 0.0), axis=1, keepdims=True
        )
        * scale
    )
    top = jnp.maximum(jnp.max(jnp.where(live, scores, -jnp.inf), axis=1, keepdims=True), own)
    probs = jnp.where(live, jnp.exp(scores - top), 0.0)
    self_prob = jnp.exp(own - top)
    total = jnp.sum(probs, axis=1, keepdims=True) + self_prob
    weights = (probs / total).astype(BF16)
    self_weight = (self_prob / total).astype(BF16).astype(F32)
    mixed = matmul(weights, vv[...].reshape(slots * ctx, width))
    mixed = mixed + self_weight * matmul(expand, fresh_value)
    mixed = jnp.where(head_mask, mixed, 0.0).astype(BF16)
    hbuf[me_g] = matmul(collapse, mixed).astype(BF16)
    copies = [
        remote(hbuf.at[me_g], hbuf.at[me_g], h_sems, (k - 1,), g_id(k)) for k in range(1, ng)
    ]
    for c in copies:
        c.start()
    pending += copies
    o_copy.wait()
    for c in copies:
        c.wait_recv()
    heads_out = hbuf[...].astype(F32).reshape(batch, width).astype(BF16)
    heads_out = matmul_tn(to_slots, heads_out).astype(BF16)

    ocols = min(COLUMNS, feat)

    def out_step(c, carry):
        at = pl.ds(pl.multiple_of(c * ocols, ocols), ocols)
        term = matmul(heads_out, wo[:, at])
        for t in range(nt):
            obuf[t, :, at] = term[t * xb : (t + 1) * xb].astype(BF16)
        return carry

    lax.fori_loop(0, feat // ocols, out_step, 0)
    copies = [
        remote(obuf.at[t_peer(k)], robuf.at[k - 1], o_sems, (k - 1,), t_id(k))
        for k in range(1, nt)
    ]
    for c in copies:
        c.start()
    pending += copies
    for c in copies:
        c.wait_recv()
    head_sums = obuf[me_t].astype(F32)
    for k in range(nt - 1):
        head_sums = head_sums + robuf[k].astype(F32)
    attended = (xv[...].astype(F32) + head_sums).astype(BF16)
    att_ref[...] = attended
    abuf[me_t] = attended
    copies = [
        remote(abuf.at[me_t], abuf.at[me_t], a_sems, (k - 1,), t_id(k)) for k in range(1, nt)
    ]
    for c in copies:
        c.start()
    pending += copies
    small[2].wait()
    for c in copies:
        c.wait_recv()

    wide = abuf[...].astype(F32).reshape(batch, feat)
    squares = jnp.sum(wide * wide, axis=1, keepdims=True)
    for g in range(ng):
        msq_send[g] = jnp.broadcast_to(squares[g * slots : (g + 1) * slots], msq_send.shape[1:])
    msq_copies = [
        remote(msq_send.at[g_peer(k)], msq_recv.at[k - 1], msq_sems, (k - 1,), g_id(k))
        for k in range(1, ng)
    ]
    for c in msq_copies:
        c.start()
    pending += msq_copies
    gained = (wide * mgainv[...]).astype(BF16)

    m_steps = []
    for j in range(3):
        m_copies[j].wait()

        def mix_step(c, carry, j=j):
            at = pl.ds(pl.multiple_of(c * cols, cols), cols)
            weight = wm[:, at] if j == 0 else wa[j - 1, :, at]
            term = matmul(gained, weight)
            for g in range(ng):
                mbuf[g, j, :, at] = term[g * slots : (g + 1) * slots].astype(BF16)
            return carry

        lax.fori_loop(0, width // cols, mix_step, 0)
        step = [
            remote(mbuf.at[g_peer(k), j], rmbuf.at[k - 1, j], m_sems, (k - 1, j), g_id(k))
            for k in range(1, ng)
        ]
        for c in step:
            c.start()
        m_steps.append(step)
        pending += step

    for c in small[5:]:
        c.wait()
    for c in msq_copies:
        c.wait_recv()
    squares = msq_send[me_g]
    for k in range(ng - 1):
        squares = squares + msq_recv[k]
    scale_rows = lax.rsqrt(squares[:, :1] / total_feat + 1e-05)
    conv = []
    for j in range(3):
        for c in m_steps[j]:
            c.wait_recv()
        total = mbuf[me_g, j].astype(F32)
        for k in range(ng - 1):
            total = total + rmbuf[k, j].astype(F32)
        conv.append(
            otv[0, j : j + 1] * (total * scale_rows)
            + otv[1, j : j + 1] * osv[0, j].astype(F32)
            + otv[2, j : j + 1] * osv[1, j].astype(F32)
        )
    product = conv[0] * conv[2]
    filtered = (
        itv[0:1] * product + itv[1:2] * isv[0].astype(F32) + itv[2:3] * isv[1].astype(F32)
    )
    gated_ref[...] = (conv[1] * filtered).astype(BF16)
    for c in pending:
        c.wait_send()


def local(
    nt,
    nr,
    nc,
    residual,
    attn_gain,
    attn_proj,
    cache_keys,
    cache_values,
    lengths,
    placement,
    out_proj,
    mix_gain,
    mix_proj,
    outer_taps,
    outer_state,
    inner_taps,
    inner_state,
):
    ng = nr * nc
    xb, feat = residual.shape
    slots = lengths.shape[0]
    batch = placement.shape[0]
    width = attn_proj.shape[2]
    anywhere = pl.BlockSpec(memory_space=pl.ANY)
    vmem = pl.BlockSpec(memory_space=pltpu.VMEM)
    dma = pltpu.SemaphoreType.DMA
    others_g, others_t = max(ng - 1, 1), max(nt - 1, 1)
    weight_values = attn_proj.size + out_proj.size + mix_proj.size
    return pl.pallas_call(
        functools.partial(kernel, nt, nr, nc),
        out_shape=(
            jax.ShapeDtypeStruct((xb, feat), BF16),
            jax.ShapeDtypeStruct((slots, width), BF16),
        ),
        in_specs=[anywhere] * 5 + [vmem] * 2 + [anywhere] * 7,
        out_specs=(vmem, vmem),
        scratch_shapes=[
            pltpu.VMEM((xb, feat), BF16),
            pltpu.VMEM((1, feat), F32),
            pltpu.VMEM((1, feat), F32),
            pltpu.VMEM(attn_proj.shape, BF16),
            pltpu.VMEM(out_proj.shape, BF16),
            pltpu.VMEM(mix_proj.shape[1:], BF16),
            pltpu.VMEM(cache_keys.shape, BF16),
            pltpu.VMEM(cache_values.shape, BF16),
            pltpu.VMEM(outer_taps.shape, F32),
            pltpu.VMEM(outer_state.shape, BF16),
            pltpu.VMEM(inner_taps.shape, F32),
            pltpu.VMEM(inner_state.shape, BF16),
            pltpu.VMEM((xb, LANES), F32),
            pltpu.VMEM((others_g, xb, LANES), F32),
            pltpu.VMEM((nt, xb, feat), BF16),
            pltpu.VMEM((ng, 3, slots, width), F32),
            pltpu.VMEM((others_g, 3, slots, width), F32),
            pltpu.VMEM((ng, slots, width), BF16),
            pltpu.VMEM((nt, xb, feat), BF16),
            pltpu.VMEM((others_t, xb, feat), BF16),
            pltpu.VMEM((nt, xb, feat), BF16),
            pltpu.VMEM((ng, slots, LANES), F32),
            pltpu.VMEM((others_g, slots, LANES), F32),
            pltpu.VMEM((ng, 3, slots, width), BF16),
            pltpu.VMEM((others_g, 3, slots, width), BF16),
            dma((9,)),
            dma((7,)),
            dma((2, others_g)),
            dma((2, others_t)),
            dma((2, others_g, 3)),
            dma((2, others_g)),
            dma((2, others_t)),
            dma((2, others_t)),
            dma((2, others_g)),
            dma((2, others_g, 3)),
        ],
        compiler_params=pltpu.CompilerParams(
            collective_id=0, has_side_effects=True, vmem_limit_bytes=58 * 2**20
        ),
        cost_estimate=pl.CostEstimate(
            flops=2 * batch * weight_values, bytes_accessed=2 * weight_values, transcendentals=0
        ),
        name="hybrid_block",
    )(
        residual,
        attn_gain.reshape(1, feat),
        attn_proj,
        cache_keys,
        cache_values,
        lengths.reshape(1, slots),
        placement.reshape(1, batch),
        out_proj,
        mix_gain.reshape(1, feat),
        mix_proj,
        outer_taps,
        outer_state,
        inner_taps,
        inner_state,
    )


def solution(mesh):
    return jax.shard_map(
        functools.partial(local, mesh.shape["tensor"], mesh.shape["rows"], mesh.shape["role"]),
        mesh=mesh,
        in_specs=(
            P(("groups", "tensor"), ("rows", "role")),
            P(("rows", "role")),
            P(None, ("rows", "role"), "tensor"),
            P(("groups", "rows", "role"), None, "tensor"),
            P(("groups", "rows", "role"), None, "tensor"),
            P(("groups", "rows", "role")),
            P("groups"),
            P("tensor", ("rows", "role")),
            P(("rows", "role")),
            P(None, ("rows", "role"), "tensor"),
            P(None, None, "tensor"),
            P(None, None, ("groups", "rows", "role"), "tensor"),
            P(None, "tensor"),
            P(None, ("groups", "rows", "role"), "tensor"),
        ),
        out_specs=(
            P(("groups", "tensor"), ("rows", "role")),
            P(("groups", "rows", "role"), "tensor"),
        ),
        check_vma=False,
    )
```

```python
import functools
import math

import jax
import jax.numpy as jnp
from jax import lax
from jax.experimental import pallas as pl
from jax.experimental.pallas import tpu as pltpu
from jax.sharding import PartitionSpec as P

HEAD_DIM = 128
LANES = 128
COLUMNS = 1024
MESH = pl.DeviceIdType.MESH
F32 = jnp.float32
BF16 = jnp.bfloat16


def quotient(a, n):
    if n & (n - 1) == 0:
        return lax.shift_right_logical(a, jnp.int32(n.bit_length() - 1))
    return lax.div(a, jnp.int32(n))


def iota(shape, axis):
    return lax.broadcasted_iota(jnp.int32, shape, axis)


def flag(mask):
    return jnp.where(mask, 1.0, 0.0).astype(BF16)


def matmul(a, b):
    return jnp.dot(a, b, preferred_element_type=F32)


def matmul_nt(a, b):
    return lax.dot_general(a, b, (((1,), (1,)), ((), ())), preferred_element_type=F32)


def matmul_tn(a, b):
    return lax.dot_general(a, b, (((0,), (0,)), ((), ())), preferred_element_type=F32)


def kernel(
    nt,
    nr,
    nc,
    x_hbm,
    again_hbm,
    aproj_hbm,
    keys_hbm,
    vals_hbm,
    lens_ref,
    place_row_ref,
    oproj_hbm,
    mgain_hbm,
    mproj_hbm,
    otaps_hbm,
    ostate_hbm,
    itaps_hbm,
    istate_hbm,
    att_ref,
    gated_ref,
    xv,
    gainv,
    mgainv,
    wa,
    wo,
    wm,
    kv,
    vv,
    otv,
    osv,
    itv,
    isv,
    sq_send,
    sq_recv,
    nbuf,
    fbuf,
    tbuf,
    cbuf,
    sbuf,
    rbuf,
    hbuf,
    obuf,
    robuf,
    abuf,
    msq_send,
    msq_recv,
    mbuf,
    rmbuf,
    lsem,
    wsem,
    sq_sems,
    n_sems,
    f_sems,
    c_sems,
    t_sems,
    h_sems,
    o_sems,
    a_sems,
    msq_sems,
    m_sems,
):
    ng = nr * nc
    me_t = lax.axis_index("tensor")
    me_r, me_c = lax.axis_index("rows"), lax.axis_index("role")
    me_g = me_r * nc + me_c
    xb, feat = xv.shape
    width = wa.shape[2]
    slots, ctx = kv.shape[0], kv.shape[1]
    heads = width // HEAD_DIM
    batch = nt * xb
    total_feat = feat * ng

    def t_peer(k):
        return lax.rem(me_t + k, nt)

    def g_peer(k):
        return lax.rem(me_g + k, ng)

    def t_id(k):
        return {"tensor": t_peer(k)}

    def g_id(k):
        p = g_peer(k)
        return {"rows": lax.div(p, nc), "role": lax.rem(p, nc)}

    def r_peer(k):
        return lax.rem(me_r + k, nr)

    def c_peer(k):
        return lax.rem(me_c + k, nc)

    def remote(src, dst, sems, at, device):
        return pltpu.make_async_remote_copy(
            src_ref=src,
            dst_ref=dst,
            send_sem=sems.at[(0,) + at],
            recv_sem=sems.at[(1,) + at],
            device_id=device,
            device_id_type=MESH,
        )

    barrier = pltpu.get_barrier_semaphore()
    for k in range(1, nt):
        pl.semaphore_signal(barrier, inc=1, device_id=t_id(k), device_id_type=MESH)
    for k in range(1, ng):
        pl.semaphore_signal(barrier, inc=1, device_id=g_id(k), device_id_type=MESH)

    small = [
        pltpu.make_async_copy(s, d, lsem.at[i])
        for i, (s, d) in enumerate(
            [
                (x_hbm, xv),
                (again_hbm, gainv),
                (mgain_hbm, mgainv),
                (keys_hbm, kv),
                (vals_hbm, vv),
                (otaps_hbm, otv),
                (ostate_hbm, osv),
                (itaps_hbm, itv),
                (istate_hbm, isv),
            ]
        )
    ]
    a_copies = [pltpu.make_async_copy(aproj_hbm.at[j], wa.at[j], wsem.at[j]) for j in range(3)]
    o_copy = pltpu.make_async_copy(oproj_hbm, wo, wsem.at[3])
    m_homes = [wm, wa.at[0], wa.at[1]]
    m_copies = [
        pltpu.make_async_copy(mproj_hbm.at[j], m_homes[j], wsem.at[4 + j]) for j in range(3)
    ]
    small[0].start()
    small[1].start()
    for c in a_copies:
        c.start()
    for c in small[2:5]:
        c.start()

    small[0].wait()
    x = xv[...].astype(F32)
    sq_send[...] = jnp.broadcast_to(jnp.sum(x * x, axis=1, keepdims=True), sq_send.shape)
    nbuf[me_t] = xv[...]
    pl.semaphore_wait(barrier, (nt - 1) + (ng - 1))
    pending = []
    copies = [remote(sq_send, sq_recv.at[k - 1], sq_sems, (k - 1,), g_id(k)) for k in range(1, ng)]
    n_copies = [remote(xv, nbuf.at[me_t], n_sems, (k - 1,), t_id(k)) for k in range(1, nt)]
    for c in copies + n_copies:
        c.start()
    pending += copies + n_copies
    place_row = place_row_ref[...]
    to_slots = flag(place_row == iota((batch, batch), 0))
    for c in copies:
        c.wait_recv()
    squares = sq_send[...]
    for k in range(ng - 1):
        squares = squares + sq_recv[k]
    fbuf[me_t] = lax.rsqrt(squares / total_feat + 1e-05)
    f_copies = [
        remote(fbuf.at[me_t], fbuf.at[me_t], f_sems, (k - 1,), t_id(k)) for k in range(1, nt)
    ]
    for c in f_copies:
        c.start()
    pending += f_copies
    small[1].wait()
    for c in n_copies + f_copies:
        c.wait_recv()
    o_copy.start()
    m_copies[0].start()
    for c in small[5:]:
        c.start()
    factors = fbuf[...].reshape(batch, LANES)[:, :1]
    normed = nbuf[...].astype(F32).reshape(batch, feat) * factors * gainv[...]
    normed = matmul(to_slots, normed.astype(BF16)).astype(BF16)

    cols = math.gcd(COLUMNS, width)

    def exchange_chips(j):
        for c in c_copies[j]:
            c.wait_recv()
        total = tbuf[j, me_c]
        for k in range(nc - 1):
            total = total + cbuf[k, j]
        sbuf[j] = total
        step = [
            remote(sbuf.at[j, r_peer(k)], rbuf.at[k - 1, j], t_sems, (k - 1, j), {"rows": r_peer(k)})
            for k in range(1, nr)
        ]
        for c in step:
            c.start()
        return step

    c_copies, t_copies = [], []
    for j in range(3):
        a_copies[j].wait()

        def attn_step(c, carry, j=j):
            at = pl.ds(pl.multiple_of(c * cols, cols), cols)
            term = matmul(normed, wa[j, :, at])
            for g in range(ng):
                tbuf[j, g % nc, g // nc, :, at] = term[g * slots : (g + 1) * slots]
            return carry

        lax.fori_loop(0, width // cols, attn_step, 0)
        if j < 2:
            m_copies[1 + j].start()
        step = [
            remote(tbuf.at[j, c_peer(k)], cbuf.at[k - 1, j], c_sems, (k - 1, j), {"role": c_peer(k)})
            for k in range(1, nc)
        ]
        for c in step:
            c.start()
        c_copies.append(step)
        pending += step
        if j > 0:
            t_copies.append(exchange_chips(j - 1))
    t_copies.append(exchange_chips(2))
    for step in t_copies:
        pending += step

    def projected(j):
        for c in t_copies[j]:
            c.wait_recv()
        total = sbuf[j, me_r]
        for k in range(nr - 1):
            total = total + rbuf[k, j]
        return total.astype(BF16)

    rows = slots * heads
    expand_mask = quotient(iota((rows, slots), 0), heads) == iota((rows, slots), 1)
    expand = flag(expand_mask)
    collapse = flag(quotient(iota((slots, rows), 1), heads) == iota((slots, rows), 0))
    row_at = iota((rows, width), 0)
    head_mask = quotient(iota((rows, width), 1), HEAD_DIM) == row_at - heads * quotient(row_at, heads)
    row_at = iota((rows, slots * ctx), 0)
    col_at = iota((rows, slots * ctx), 1)
    col_slot = quotient(col_at, ctx)
    row_length = jnp.sum(
        jnp.where(expand_mask, lens_ref[...].astype(F32), 0.0), axis=1, keepdims=True
    )
    live = (quotient(row_at, heads) == col_slot) & (
        (col_at - ctx * col_slot).astype(F32) < row_length
    )

    small[3].wait()
    small[4].wait()

    scale = 1.0 / math.sqrt(HEAD_DIM)
    spread = jnp.where(head_mask, matmul(expand, projected(0)), 0.0).astype(BF16)
    scores = matmul_nt(spread, kv[...].reshape(slots * ctx, width)) * scale
    own = (
        jnp.sum(
            jnp.where(expand_mask, matmul_nt(spread, projected(1)), 0.0), axis=1, keepdims=True
        )
        * scale
    )
    top = jnp.maximum(jnp.max(jnp.where(live, scores, -jnp.inf), axis=1, keepdims=True), own)
    probs = jnp.where(live, jnp.exp(scores - top), 0.0)
    self_prob = jnp.exp(own - top)
    total = jnp.sum(probs, axis=1, keepdims=True) + self_prob
    weights = (probs / total).astype(BF16)
    self_weight = (self_prob / total).astype(BF16).astype(F32)
    mixed = matmul(weights, vv[...].reshape(slots * ctx, width))
    mixed = mixed + self_weight * matmul(expand, projected(2))
    mixed = jnp.where(head_mask, mixed, 0.0).astype(BF16)
    hbuf[me_g] = matmul(collapse, mixed).astype(BF16)
    copies = [
        remote(hbuf.at[me_g], hbuf.at[me_g], h_sems, (k - 1,), g_id(k)) for k in range(1, ng)
    ]
    for c in copies:
        c.start()
    pending += copies
    o_copy.wait()
    for c in copies:
        c.wait_recv()
    heads_out = hbuf[...].astype(F32).reshape(batch, width).astype(BF16)
    heads_out = matmul_tn(to_slots, heads_out).astype(BF16)

    pieces, ocols = obuf.shape[0], obuf.shape[3]
    o_copies, a_out = [], []
    for p in range(pieces):
        term = matmul(heads_out, wo[:, p * ocols : (p + 1) * ocols])
        for t in range(nt):
            obuf[p, t] = term[t * xb : (t + 1) * xb].astype(BF16)
        step = [
            remote(obuf.at[p, t_peer(k)], robuf.at[p, k - 1], o_sems, (p, k - 1), t_id(k))
            for k in range(1, nt)
        ]
        for c in step:
            c.start()
        o_copies.append(step)
        pending += step
    for p in range(pieces):
        for c in o_copies[p]:
            c.wait_recv()
        head_sums = obuf[p, me_t].astype(F32)
        for k in range(nt - 1):
            head_sums = head_sums + robuf[p, k].astype(F32)
        at = slice(p * ocols, (p + 1) * ocols)
        attended = (xv[:, at].astype(F32) + head_sums).astype(BF16)
        att_ref[:, at] = attended
        abuf[p, me_t] = attended
        step = [
            remote(abuf.at[p, me_t], abuf.at[p, me_t], a_sems, (p, k - 1), t_id(k))
            for k in range(1, nt)
        ]
        for c in step:
            c.start()
        a_out.append(step)
        pending += step
    small[2].wait()

    gained, squares = [], 0.0
    for p in range(pieces):
        for c in a_out[p]:
            c.wait_recv()
        wide = abuf[p].astype(F32).reshape(batch, ocols)
        squares = squares + jnp.sum(wide * wide, axis=1, keepdims=True)
        gained.append((wide * mgainv[:, p * ocols : (p + 1) * ocols]).astype(BF16))
    gained = jnp.concatenate(gained, axis=1)
    for g in range(ng):
        msq_send[g] = jnp.broadcast_to(squares[g * slots : (g + 1) * slots], msq_send.shape[1:])
    msq_copies = [
        remote(msq_send.at[g_peer(k)], msq_recv.at[k - 1], msq_sems, (k - 1,), g_id(k))
        for k in range(1, ng)
    ]
    for c in msq_copies:
        c.start()
    pending += msq_copies

    m_steps = []
    for j in range(3):
        m_copies[j].wait()

        def mix_step(c, carry, j=j):
            at = pl.ds(pl.multiple_of(c * cols, cols), cols)
            weight = wm[:, at] if j == 0 else wa[j - 1, :, at]
            term = matmul(gained, weight)
            for g in range(ng):
                mbuf[g, j, :, at] = term[g * slots : (g + 1) * slots].astype(BF16)
            return carry

        lax.fori_loop(0, width // cols, mix_step, 0)
        step = [
            remote(mbuf.at[g_peer(k), j], rmbuf.at[k - 1, j], m_sems, (k - 1, j), g_id(k))
            for k in range(1, ng)
        ]
        for c in step:
            c.start()
        m_steps.append(step)
        pending += step

    for c in small[5:]:
        c.wait()
    for c in msq_copies:
        c.wait_recv()
    squares = msq_send[me_g]
    for k in range(ng - 1):
        squares = squares + msq_recv[k]
    scale_rows = lax.rsqrt(squares[:, :1] / total_feat + 1e-05)
    conv = []
    for j in range(3):
        for c in m_steps[j]:
            c.wait_recv()
        total = mbuf[me_g, j].astype(F32)
        for k in range(ng - 1):
            total = total + rmbuf[k, j].astype(F32)
        conv.append(
            otv[0, j : j + 1] * (total * scale_rows)
            + otv[1, j : j + 1] * osv[0, j].astype(F32)
            + otv[2, j : j + 1] * osv[1, j].astype(F32)
        )
    product = conv[0] * conv[2]
    filtered = (
        itv[0:1] * product + itv[1:2] * isv[0].astype(F32) + itv[2:3] * isv[1].astype(F32)
    )
    gated_ref[...] = (conv[1] * filtered).astype(BF16)
    for c in pending:
        c.wait_send()


def local(
    nt,
    nr,
    nc,
    residual,
    attn_gain,
    attn_proj,
    cache_keys,
    cache_values,
    lengths,
    placement,
    out_proj,
    mix_gain,
    mix_proj,
    outer_taps,
    outer_state,
    inner_taps,
    inner_state,
):
    ng = nr * nc
    xb, feat = residual.shape
    slots = lengths.shape[0]
    batch = placement.shape[0]
    width = attn_proj.shape[2]
    anywhere = pl.BlockSpec(memory_space=pl.ANY)
    vmem = pl.BlockSpec(memory_space=pltpu.VMEM)
    dma = pltpu.SemaphoreType.DMA
    others_g, others_t = max(ng - 1, 1), max(nt - 1, 1)
    others_r, others_c = max(nr - 1, 1), max(nc - 1, 1)
    ocols = math.gcd(COLUMNS, feat)
    pieces = feat // ocols
    weight_values = attn_proj.size + out_proj.size + mix_proj.size
    return pl.pallas_call(
        functools.partial(kernel, nt, nr, nc),
        out_shape=(
            jax.ShapeDtypeStruct((xb, feat), BF16),
            jax.ShapeDtypeStruct((slots, width), BF16),
        ),
        in_specs=[anywhere] * 5 + [vmem] * 2 + [anywhere] * 7,
        out_specs=(vmem, vmem),
        scratch_shapes=[
            pltpu.VMEM((xb, feat), BF16),
            pltpu.VMEM((1, feat), F32),
            pltpu.VMEM((1, feat), F32),
            pltpu.VMEM(attn_proj.shape, BF16),
            pltpu.VMEM(out_proj.shape, BF16),
            pltpu.VMEM(mix_proj.shape[1:], BF16),
            pltpu.VMEM(cache_keys.shape, BF16),
            pltpu.VMEM(cache_values.shape, BF16),
            pltpu.VMEM(outer_taps.shape, F32),
            pltpu.VMEM(outer_state.shape, BF16),
            pltpu.VMEM(inner_taps.shape, F32),
            pltpu.VMEM(inner_state.shape, BF16),
            pltpu.VMEM((xb, LANES), F32),
            pltpu.VMEM((others_g, xb, LANES), F32),
            pltpu.VMEM((nt, xb, feat), BF16),
            pltpu.VMEM((nt, xb, LANES), F32),
            pltpu.VMEM((3, nc, nr, slots, width), F32),
            pltpu.VMEM((others_c, 3, nr, slots, width), F32),
            pltpu.VMEM((3, nr, slots, width), F32),
            pltpu.VMEM((others_r, 3, slots, width), F32),
            pltpu.VMEM((ng, slots, width), BF16),
            pltpu.VMEM((pieces, nt, xb, ocols), BF16),
            pltpu.VMEM((pieces, others_t, xb, ocols), BF16),
            pltpu.VMEM((pieces, nt, xb, ocols), BF16),
            pltpu.VMEM((ng, slots, LANES), F32),
            pltpu.VMEM((others_g, slots, LANES), F32),
            pltpu.VMEM((ng, 3, slots, width), BF16),
            pltpu.VMEM((others_g, 3, slots, width), BF16),
            dma((9,)),
            dma((7,)),
            dma((2, others_g)),
            dma((2, others_t)),
            dma((2, others_t)),
            dma((2, others_c, 3)),
            dma((2, others_r, 3)),
            dma((2, others_g)),
            dma((2, pieces, others_t)),
            dma((2, pieces, others_t)),
            dma((2, others_g)),
            dma((2, others_g, 3)),
        ],
        compiler_params=pltpu.CompilerParams(
            collective_id=0, has_side_effects=True, vmem_limit_bytes=58 * 2**20
        ),
        cost_estimate=pl.CostEstimate(
            flops=2 * batch * weight_values, bytes_accessed=2 * weight_values, transcendentals=0
        ),
        name="hybrid_block",
    )(
        residual,
        attn_gain.reshape(1, feat),
        attn_proj,
        cache_keys,
        cache_values,
        lengths.reshape(1, slots),
        placement.reshape(1, batch),
        out_proj,
        mix_gain.reshape(1, feat),
        mix_proj,
        outer_taps,
        outer_state,
        inner_taps,
        inner_state,
    )


def solution(mesh):
    return jax.shard_map(
        functools.partial(local, mesh.shape["tensor"], mesh.shape["rows"], mesh.shape["role"]),
        mesh=mesh,
        in_specs=(
            P(("groups", "tensor"), ("rows", "role")),
            P(("rows", "role")),
            P(None, ("rows", "role"), "tensor"),
            P(("groups", "rows", "role"), None, "tensor"),
            P(("groups", "rows", "role"), None, "tensor"),
            P(("groups", "rows", "role")),
            P("groups"),
            P("tensor", ("rows", "role")),
            P(("rows", "role")),
            P(None, ("rows", "role"), "tensor"),
            P(None, None, "tensor"),
            P(None, None, ("groups", "rows", "role"), "tensor"),
            P(None, "tensor"),
            P(None, ("groups", "rows", "role"), "tensor"),
        ),
        out_specs=(
            P(("groups", "tensor"), ("rows", "role")),
            P(("groups", "rows", "role"), "tensor"),
        ),
        check_vma=False,
    )
```

```python
import functools
import math

import jax
import jax.numpy as jnp
from jax import lax
from jax.experimental import pallas as pl
from jax.experimental.pallas import tpu as pltpu
from jax.sharding import PartitionSpec as P

HEAD_DIM = 128
LANES = 128
COLUMNS = 1024
MESH = pl.DeviceIdType.MESH
F32 = jnp.float32
BF16 = jnp.bfloat16


def quotient(a, n):
    if n & (n - 1) == 0:
        return lax.shift_right_logical(a, jnp.int32(n.bit_length() - 1))
    return lax.div(a, jnp.int32(n))


def iota(shape, axis):
    return lax.broadcasted_iota(jnp.int32, shape, axis)


def flag(mask):
    return jnp.where(mask, 1.0, 0.0).astype(BF16)


def matmul(a, b):
    return jnp.dot(a, b, preferred_element_type=F32)


def matmul_nt(a, b):
    return lax.dot_general(a, b, (((1,), (1,)), ((), ())), preferred_element_type=F32)


def matmul_tn(a, b):
    return lax.dot_general(a, b, (((0,), (0,)), ((), ())), preferred_element_type=F32)


def kernel(
    nt,
    nr,
    nc,
    x_hbm,
    again_hbm,
    aproj_hbm,
    keys_hbm,
    vals_hbm,
    lens_ref,
    place_row_ref,
    oproj_hbm,
    mgain_hbm,
    mproj_hbm,
    otaps_hbm,
    ostate_hbm,
    itaps_hbm,
    istate_hbm,
    att_ref,
    gated_ref,
    xv,
    gainv,
    mgainv,
    wa,
    wo,
    wm,
    kv,
    vv,
    otv,
    osv,
    itv,
    isv,
    sq_send,
    sq_recv,
    nbuf,
    fbuf,
    tbuf,
    cbuf,
    sbuf,
    rbuf,
    hbuf,
    obuf,
    robuf,
    abuf,
    msq_send,
    msq_recv,
    macc,
    mbuf,
    mcbuf,
    msbuf,
    rmbuf,
    lsem,
    wsem,
    sq_sems,
    n_sems,
    f_sems,
    c_sems,
    t_sems,
    h_sems,
    o_sems,
    a_sems,
    msq_sems,
    mc_sems,
    m_sems,
):
    ng = nr * nc
    me_t = lax.axis_index("tensor")
    me_r, me_c = lax.axis_index("rows"), lax.axis_index("role")
    me_g = me_r * nc + me_c
    xb, feat = xv.shape
    width = wa.shape[2]
    slots, ctx = kv.shape[0], kv.shape[1]
    heads = width // HEAD_DIM
    batch = nt * xb
    total_feat = feat * ng

    def t_peer(k):
        return lax.rem(me_t + k, nt)

    def g_peer(k):
        return lax.rem(me_g + k, ng)

    def t_id(k):
        return {"tensor": t_peer(k)}

    def g_id(k):
        p = g_peer(k)
        return {"rows": lax.div(p, nc), "role": lax.rem(p, nc)}

    def r_peer(k):
        return lax.rem(me_r + k, nr)

    def c_peer(k):
        return lax.rem(me_c + k, nc)

    def remote(src, dst, sems, at, device):
        return pltpu.make_async_remote_copy(
            src_ref=src,
            dst_ref=dst,
            send_sem=sems.at[(0,) + at],
            recv_sem=sems.at[(1,) + at],
            device_id=device,
            device_id_type=MESH,
        )

    barrier = pltpu.get_barrier_semaphore()
    for k in range(1, nt):
        pl.semaphore_signal(barrier, inc=1, device_id=t_id(k), device_id_type=MESH)
    for k in range(1, ng):
        pl.semaphore_signal(barrier, inc=1, device_id=g_id(k), device_id_type=MESH)

    small = [
        pltpu.make_async_copy(s, d, lsem.at[i])
        for i, (s, d) in enumerate(
            [
                (x_hbm, xv),
                (again_hbm, gainv),
                (mgain_hbm, mgainv),
                (keys_hbm, kv),
                (vals_hbm, vv),
                (otaps_hbm, otv),
                (ostate_hbm, osv),
                (itaps_hbm, itv),
                (istate_hbm, isv),
            ]
        )
    ]
    a_copies = [pltpu.make_async_copy(aproj_hbm.at[j], wa.at[j], wsem.at[j]) for j in range(3)]
    o_copy = pltpu.make_async_copy(oproj_hbm, wo, wsem.at[3])
    m_homes = [wm, wa.at[0], wa.at[1]]
    m_copies = [
        pltpu.make_async_copy(mproj_hbm.at[j], m_homes[j], wsem.at[4 + j]) for j in range(3)
    ]
    small[0].start()
    small[1].start()
    for c in a_copies:
        c.start()
    for c in small[2:5]:
        c.start()

    small[0].wait()
    x = xv[...].astype(F32)
    sq_send[...] = jnp.broadcast_to(jnp.sum(x * x, axis=1, keepdims=True), sq_send.shape)
    nbuf[me_t] = xv[...]
    pl.semaphore_wait(barrier, (nt - 1) + (ng - 1))
    pending = []
    copies = [remote(sq_send, sq_recv.at[k - 1], sq_sems, (k - 1,), g_id(k)) for k in range(1, ng)]
    n_copies = [remote(xv, nbuf.at[me_t], n_sems, (k - 1,), t_id(k)) for k in range(1, nt)]
    for c in copies + n_copies:
        c.start()
    pending += copies + n_copies
    place_row = place_row_ref[...]
    to_slots = flag(place_row == iota((batch, batch), 0))
    for c in copies:
        c.wait_recv()
    squares = sq_send[...]
    for k in range(ng - 1):
        squares = squares + sq_recv[k]
    fbuf[me_t] = lax.rsqrt(squares / total_feat + 1e-05)
    f_copies = [
        remote(fbuf.at[me_t], fbuf.at[me_t], f_sems, (k - 1,), t_id(k)) for k in range(1, nt)
    ]
    for c in f_copies:
        c.start()
    pending += f_copies
    small[1].wait()
    for c in n_copies + f_copies:
        c.wait_recv()
    o_copy.start()
    m_copies[0].start()
    for c in small[5:]:
        c.start()
    factors = fbuf[...].reshape(batch, LANES)[:, :1]
    normed = nbuf[...].astype(F32).reshape(batch, feat) * factors * gainv[...]
    normed = matmul(to_slots, normed.astype(BF16)).astype(BF16)

    cols = math.gcd(COLUMNS, width)

    def exchange_chips(j):
        for c in c_copies[j]:
            c.wait_recv()
        total = tbuf[j, me_c]
        for k in range(nc - 1):
            total = total + cbuf[k, j]
        sbuf[j] = total
        step = [
            remote(sbuf.at[j, r_peer(k)], rbuf.at[k - 1, j], t_sems, (k - 1, j), {"rows": r_peer(k)})
            for k in range(1, nr)
        ]
        for c in step:
            c.start()
        return step

    c_copies, t_copies = [], []
    for j in range(3):
        a_copies[j].wait()

        def attn_step(c, carry, j=j):
            at = pl.ds(pl.multiple_of(c * cols, cols), cols)
            term = matmul(normed, wa[j, :, at])
            for g in range(ng):
                tbuf[j, g % nc, g // nc, :, at] = term[g * slots : (g + 1) * slots]
            return carry

        lax.fori_loop(0, width // cols, attn_step, 0)
        if j < 2:
            m_copies[1 + j].start()
        step = [
            remote(tbuf.at[j, c_peer(k)], cbuf.at[k - 1, j], c_sems, (k - 1, j), {"role": c_peer(k)})
            for k in range(1, nc)
        ]
        for c in step:
            c.start()
        c_copies.append(step)
        pending += step
        if j > 0:
            t_copies.append(exchange_chips(j - 1))
    t_copies.append(exchange_chips(2))
    for step in t_copies:
        pending += step

    def projected(j):
        for c in t_copies[j]:
            c.wait_recv()
        total = sbuf[j, me_r]
        for k in range(nr - 1):
            total = total + rbuf[k, j]
        return total.astype(BF16)

    rows = slots * heads
    expand_mask = quotient(iota((rows, slots), 0), heads) == iota((rows, slots), 1)
    expand = flag(expand_mask)
    collapse = flag(quotient(iota((slots, rows), 1), heads) == iota((slots, rows), 0))
    row_at = iota((rows, width), 0)
    head_mask = quotient(iota((rows, width), 1), HEAD_DIM) == row_at - heads * quotient(row_at, heads)
    row_at = iota((rows, slots * ctx), 0)
    col_at = iota((rows, slots * ctx), 1)
    col_slot = quotient(col_at, ctx)
    row_length = jnp.sum(
        jnp.where(expand_mask, lens_ref[...].astype(F32), 0.0), axis=1, keepdims=True
    )
    live = (quotient(row_at, heads) == col_slot) & (
        (col_at - ctx * col_slot).astype(F32) < row_length
    )

    small[3].wait()
    small[4].wait()

    scale = 1.0 / math.sqrt(HEAD_DIM)
    spread = jnp.where(head_mask, matmul(expand, projected(0)), 0.0).astype(BF16)
    scores = matmul_nt(spread, kv[...].reshape(slots * ctx, width)) * scale
    own = (
        jnp.sum(
            jnp.where(expand_mask, matmul_nt(spread, projected(1)), 0.0), axis=1, keepdims=True
        )
        * scale
    )
    top = jnp.maximum(jnp.max(jnp.where(live, scores, -jnp.inf), axis=1, keepdims=True), own)
    probs = jnp.where(live, jnp.exp(scores - top), 0.0)
    self_prob = jnp.exp(own - top)
    total = jnp.sum(probs, axis=1, keepdims=True) + self_prob
    weights = (probs / total).astype(BF16)
    self_weight = (self_prob / total).astype(BF16).astype(F32)
    mixed = matmul(weights, vv[...].reshape(slots * ctx, width))
    mixed = mixed + self_weight * matmul(expand, projected(2))
    mixed = jnp.where(head_mask, mixed, 0.0).astype(BF16)
    hbuf[me_g] = matmul(collapse, mixed).astype(BF16)
    copies = [
        remote(hbuf.at[me_g], hbuf.at[me_g], h_sems, (k - 1,), g_id(k)) for k in range(1, ng)
    ]
    for c in copies:
        c.start()
    pending += copies
    o_copy.wait()
    for c in copies:
        c.wait_recv()
    heads_out = hbuf[...].astype(F32).reshape(batch, width).astype(BF16)
    heads_out = matmul_tn(to_slots, heads_out).astype(BF16)

    pieces, ocols = obuf.shape[0], obuf.shape[3]
    o_copies, a_out = [], []
    for p in range(pieces):
        term = matmul(heads_out, wo[:, p * ocols : (p + 1) * ocols])
        for t in range(nt):
            obuf[p, t] = term[t * xb : (t + 1) * xb].astype(BF16)
        step = [
            remote(obuf.at[p, t_peer(k)], robuf.at[p, k - 1], o_sems, (p, k - 1), t_id(k))
            for k in range(1, nt)
        ]
        for c in step:
            c.start()
        o_copies.append(step)
        pending += step
    for p in range(pieces):
        for c in o_copies[p]:
            c.wait_recv()
        head_sums = obuf[p, me_t].astype(F32)
        for k in range(nt - 1):
            head_sums = head_sums + robuf[p, k].astype(F32)
        at = slice(p * ocols, (p + 1) * ocols)
        attended = (xv[:, at].astype(F32) + head_sums).astype(BF16)
        att_ref[:, at] = attended
        abuf[p, me_t] = attended
        step = [
            remote(abuf.at[p, me_t], abuf.at[p, me_t], a_sems, (p, k - 1), t_id(k))
            for k in range(1, nt)
        ]
        for c in step:
            c.start()
        a_out.append(step)
        pending += step
    small[2].wait()

    def mix_weight(j):
        return wm if j == 0 else wa.at[j - 1]

    def cross_chips(j):
        for c in mc_copies[j]:
            c.wait_recv()
        total = mbuf[j, me_c].astype(F32)
        for k in range(nc - 1):
            total = total + mcbuf[k, j].astype(F32)
        msbuf[j] = total.astype(BF16)
        step = [
            remote(
                msbuf.at[j, r_peer(k)], rmbuf.at[k - 1, j], m_sems, (k - 1, j), {"rows": r_peer(k)}
            )
            for k in range(1, nr)
        ]
        for c in step:
            c.start()
        return step

    squares = 0.0
    mc_copies, m_steps = [], []
    for p in range(pieces):
        for c in a_out[p]:
            c.wait_recv()
        depth = slice(p * ocols, (p + 1) * ocols)
        wide = abuf[p].astype(F32).reshape(batch, ocols)
        squares = squares + jnp.sum(wide * wide, axis=1, keepdims=True)
        gained = (wide * mgainv[:, depth]).astype(BF16)
        last = p == pieces - 1
        if last:
            for g in range(ng):
                msq_send[g] = jnp.broadcast_to(
                    squares[g * slots : (g + 1) * slots], msq_send.shape[1:]
                )
            msq_copies = [
                remote(msq_send.at[g_peer(k)], msq_recv.at[k - 1], msq_sems, (k - 1,), g_id(k))
                for k in range(1, ng)
            ]
            for c in msq_copies:
                c.start()
            pending += msq_copies
        for j in range(3):
            if p == 0:
                m_copies[j].wait()

            def mix_step(c, carry, p=p, j=j, last=last, depth=depth, gained=gained):
                at = pl.ds(pl.multiple_of(c * cols, cols), cols)
                term = matmul(gained, mix_weight(j)[depth, at])
                if p > 0:
                    term = term + macc[j, :, at]
                if last:
                    for g in range(ng):
                        mbuf[j, g % nc, g // nc, :, at] = term[
                            g * slots : (g + 1) * slots
                        ].astype(BF16)
                else:
                    macc[j, :, at] = term
                return carry

            lax.fori_loop(0, width // cols, mix_step, 0)
            if last:
                step = [
                    remote(
                        mbuf.at[j, c_peer(k)],
                        mcbuf.at[k - 1, j],
                        mc_sems,
                        (k - 1, j),
                        {"role": c_peer(k)},
                    )
                    for k in range(1, nc)
                ]
                for c in step:
                    c.start()
                mc_copies.append(step)
                pending += step
                if j > 0:
                    m_steps.append(cross_chips(j - 1))
    m_steps.append(cross_chips(2))
    for step in m_steps:
        pending += step

    for c in small[5:]:
        c.wait()
    for c in msq_copies:
        c.wait_recv()
    squares = msq_send[me_g]
    for k in range(ng - 1):
        squares = squares + msq_recv[k]
    scale_rows = lax.rsqrt(squares[:, :1] / total_feat + 1e-05)
    conv = []
    for j in range(3):
        for c in m_steps[j]:
            c.wait_recv()
        total = msbuf[j, me_r].astype(F32)
        for k in range(nr - 1):
            total = total + rmbuf[k, j].astype(F32)
        conv.append(
            otv[0, j : j + 1] * (total * scale_rows)
            + otv[1, j : j + 1] * osv[0, j].astype(F32)
            + otv[2, j : j + 1] * osv[1, j].astype(F32)
        )
    product = conv[0] * conv[2]
    filtered = (
        itv[0:1] * product + itv[1:2] * isv[0].astype(F32) + itv[2:3] * isv[1].astype(F32)
    )
    gated_ref[...] = (conv[1] * filtered).astype(BF16)
    for c in pending:
        c.wait_send()


def hand_over(att_in, gated_in, att_out, gated_out, sems):
    copies = [
        pltpu.make_async_copy(att_in, att_out, sems.at[0]),
        pltpu.make_async_copy(gated_in, gated_out, sems.at[1]),
    ]
    for c in copies:
        c.start()
    for c in copies:
        c.wait()


def local(
    nt,
    nr,
    nc,
    residual,
    attn_gain,
    attn_proj,
    cache_keys,
    cache_values,
    lengths,
    placement,
    out_proj,
    mix_gain,
    mix_proj,
    outer_taps,
    outer_state,
    inner_taps,
    inner_state,
):
    ng = nr * nc
    xb, feat = residual.shape
    slots = lengths.shape[0]
    batch = placement.shape[0]
    width = attn_proj.shape[2]
    anywhere = pl.BlockSpec(memory_space=pl.ANY)
    vmem = pl.BlockSpec(memory_space=pltpu.VMEM)
    dma = pltpu.SemaphoreType.DMA
    others_g, others_t = max(ng - 1, 1), max(nt - 1, 1)
    others_r, others_c = max(nr - 1, 1), max(nc - 1, 1)
    ocols = math.gcd(COLUMNS, feat)
    pieces = feat // ocols
    weight_values = attn_proj.size + out_proj.size + mix_proj.size
    attended, gated = pl.pallas_call(
        functools.partial(kernel, nt, nr, nc),
        out_shape=(
            jax.ShapeDtypeStruct((xb, feat), BF16),
            jax.ShapeDtypeStruct((slots, width), BF16),
        ),
        in_specs=[anywhere] * 5 + [vmem] * 2 + [anywhere] * 7,
        out_specs=(vmem, vmem),
        scratch_shapes=[
            pltpu.VMEM((xb, feat), BF16),
            pltpu.VMEM((1, feat), F32),
            pltpu.VMEM((1, feat), F32),
            pltpu.VMEM(attn_proj.shape, BF16),
            pltpu.VMEM(out_proj.shape, BF16),
            pltpu.VMEM(mix_proj.shape[1:], BF16),
            pltpu.VMEM(cache_keys.shape, BF16),
            pltpu.VMEM(cache_values.shape, BF16),
            pltpu.VMEM(outer_taps.shape, F32),
            pltpu.VMEM(outer_state.shape, BF16),
            pltpu.VMEM(inner_taps.shape, F32),
            pltpu.VMEM(inner_state.shape, BF16),
            pltpu.VMEM((xb, LANES), F32),
            pltpu.VMEM((others_g, xb, LANES), F32),
            pltpu.VMEM((nt, xb, feat), BF16),
            pltpu.VMEM((nt, xb, LANES), F32),
            pltpu.VMEM((3, nc, nr, slots, width), F32),
            pltpu.VMEM((others_c, 3, nr, slots, width), F32),
            pltpu.VMEM((3, nr, slots, width), F32),
            pltpu.VMEM((others_r, 3, slots, width), F32),
            pltpu.VMEM((ng, slots, width), BF16),
            pltpu.VMEM((pieces, nt, xb, ocols), BF16),
            pltpu.VMEM((pieces, others_t, xb, ocols), BF16),
            pltpu.VMEM((pieces, nt, xb, ocols), BF16),
            pltpu.VMEM((ng, slots, LANES), F32),
            pltpu.VMEM((others_g, slots, LANES), F32),
            pltpu.VMEM((3, batch, width), F32),
            pltpu.VMEM((3, nc, nr, slots, width), BF16),
            pltpu.VMEM((others_c, 3, nr, slots, width), BF16),
            pltpu.VMEM((3, nr, slots, width), BF16),
            pltpu.VMEM((others_r, 3, slots, width), BF16),
            dma((9,)),
            dma((7,)),
            dma((2, others_g)),
            dma((2, others_t)),
            dma((2, others_t)),
            dma((2, others_c, 3)),
            dma((2, others_r, 3)),
            dma((2, others_g)),
            dma((2, pieces, others_t)),
            dma((2, pieces, others_t)),
            dma((2, others_g)),
            dma((2, others_c, 3)),
            dma((2, others_r, 3)),
        ],
        compiler_params=pltpu.CompilerParams(
            collective_id=0, has_side_effects=True, vmem_limit_bytes=58 * 2**20
        ),
        cost_estimate=pl.CostEstimate(
            flops=2 * batch * weight_values, bytes_accessed=2 * weight_values, transcendentals=0
        ),
        name="hybrid_block",
    )(
        residual,
        attn_gain.reshape(1, feat),
        attn_proj,
        cache_keys,
        cache_values,
        lengths.reshape(1, slots),
        placement.reshape(1, batch),
        out_proj,
        mix_gain.reshape(1, feat),
        mix_proj,
        outer_taps,
        outer_state,
        inner_taps,
        inner_state,
    )
    return pl.pallas_call(
        hand_over,
        out_shape=(
            jax.ShapeDtypeStruct((xb, feat), BF16),
            jax.ShapeDtypeStruct((slots, width), BF16),
        ),
        in_specs=[anywhere] * 2,
        out_specs=(anywhere, anywhere),
        scratch_shapes=[dma((2,))],
        name="hand_over",
    )(attended, gated)


def solution(mesh):
    return jax.shard_map(
        functools.partial(local, mesh.shape["tensor"], mesh.shape["rows"], mesh.shape["role"]),
        mesh=mesh,
        in_specs=(
            P(("groups", "tensor"), ("rows", "role")),
            P(("rows", "role")),
            P(None, ("rows", "role"), "tensor"),
            P(("groups", "rows", "role"), None, "tensor"),
            P(("groups", "rows", "role"), None, "tensor"),
            P(("groups", "rows", "role")),
            P("groups"),
            P("tensor", ("rows", "role")),
            P(("rows", "role")),
            P(None, ("rows", "role"), "tensor"),
            P(None, None, "tensor"),
            P(None, None, ("groups", "rows", "role"), "tensor"),
            P(None, "tensor"),
            P(None, ("groups", "rows", "role"), "tensor"),
        ),
        out_specs=(
            P(("groups", "tensor"), ("rows", "role")),
            P(("groups", "rows", "role"), "tensor"),
        ),
        check_vma=False,
    )
```

```python
import functools
import math

import jax
import jax.numpy as jnp
from jax import lax
from jax.experimental import pallas as pl
from jax.experimental.pallas import tpu as pltpu
from jax.sharding import PartitionSpec as P

HEAD_DIM = 128
LANES = 128
COLUMNS = 1024
MESH = pl.DeviceIdType.MESH
F32 = jnp.float32
BF16 = jnp.bfloat16


def quotient(a, n):
    if n & (n - 1) == 0:
        return lax.shift_right_logical(a, jnp.int32(n.bit_length() - 1))
    return lax.div(a, jnp.int32(n))


def iota(shape, axis):
    return lax.broadcasted_iota(jnp.int32, shape, axis)


def flag(mask):
    return jnp.where(mask, 1.0, 0.0).astype(BF16)


def matmul(a, b):
    return jnp.dot(a, b, preferred_element_type=F32)


def matmul_nt(a, b):
    return lax.dot_general(a, b, (((1,), (1,)), ((), ())), preferred_element_type=F32)


def matmul_tn(a, b):
    return lax.dot_general(a, b, (((0,), (0,)), ((), ())), preferred_element_type=F32)


def kernel(
    nt,
    nr,
    nc,
    x_hbm,
    again_hbm,
    aproj_hbm,
    keys_hbm,
    vals_hbm,
    lens_ref,
    place_row_ref,
    oproj_hbm,
    mgain_hbm,
    mproj_hbm,
    otaps_hbm,
    ostate_hbm,
    itaps_hbm,
    istate_hbm,
    att_ref,
    gated_ref,
    xv,
    gainv,
    mgainv,
    wa,
    wo,
    wm,
    kv,
    vv,
    otv,
    osv,
    itv,
    isv,
    sq_send,
    sq_recv,
    nbuf,
    fbuf,
    tbuf,
    cbuf,
    sbuf,
    rbuf,
    hbuf,
    obuf,
    robuf,
    abuf,
    msq_send,
    msq_recv,
    mbuf,
    rmbuf,
    lsem,
    wsem,
    sq_sems,
    n_sems,
    f_sems,
    c_sems,
    t_sems,
    h_sems,
    o_sems,
    a_sems,
    msq_sems,
    m_sems,
):
    ng = nr * nc
    me_t = lax.axis_index("tensor")
    me_r, me_c = lax.axis_index("rows"), lax.axis_index("role")
    me_g = me_r * nc + me_c
    xb, feat = xv.shape
    width = wa.shape[2]
    slots, ctx = kv.shape[0], kv.shape[1]
    heads = width // HEAD_DIM
    batch = nt * xb
    total_feat = feat * ng

    def t_peer(k):
        return lax.rem(me_t + k, nt)

    def g_peer(k):
        return lax.rem(me_g + k, ng)

    def t_id(k):
        return {"tensor": t_peer(k)}

    def g_id(k):
        p = g_peer(k)
        return {"rows": lax.div(p, nc), "role": lax.rem(p, nc)}

    def r_peer(k):
        return lax.rem(me_r + k, nr)

    def c_peer(k):
        return lax.rem(me_c + k, nc)

    def remote(src, dst, sems, at, device):
        return pltpu.make_async_remote_copy(
            src_ref=src,
            dst_ref=dst,
            send_sem=sems.at[(0,) + at],
            recv_sem=sems.at[(1,) + at],
            device_id=device,
            device_id_type=MESH,
        )

    barrier = pltpu.get_barrier_semaphore()
    for k in range(1, nt):
        pl.semaphore_signal(barrier, inc=1, device_id=t_id(k), device_id_type=MESH)
    for k in range(1, ng):
        pl.semaphore_signal(barrier, inc=1, device_id=g_id(k), device_id_type=MESH)

    small = [
        pltpu.make_async_copy(s, d, lsem.at[i])
        for i, (s, d) in enumerate(
            [
                (x_hbm, xv),
                (again_hbm, gainv),
                (mgain_hbm, mgainv),
                (keys_hbm, kv),
                (vals_hbm, vv),
                (otaps_hbm, otv),
                (ostate_hbm, osv),
                (itaps_hbm, itv),
                (istate_hbm, isv),
            ]
        )
    ]
    a_copies = [pltpu.make_async_copy(aproj_hbm.at[j], wa.at[j], wsem.at[j]) for j in range(3)]
    o_copy = pltpu.make_async_copy(oproj_hbm, wo, wsem.at[3])
    m_homes = [wm, wa.at[0], wa.at[1]]
    m_copies = [
        pltpu.make_async_copy(mproj_hbm.at[j], m_homes[j], wsem.at[4 + j]) for j in range(3)
    ]
    small[0].start()
    small[1].start()
    for c in a_copies:
        c.start()
    for c in small[2:5]:
        c.start()

    small[0].wait()
    x = xv[...].astype(F32)
    sq_send[...] = jnp.broadcast_to(jnp.sum(x * x, axis=1, keepdims=True), sq_send.shape)
    nbuf[me_t] = xv[...]
    pl.semaphore_wait(barrier, (nt - 1) + (ng - 1))
    pending = []
    copies = [remote(sq_send, sq_recv.at[k - 1], sq_sems, (k - 1,), g_id(k)) for k in range(1, ng)]
    n_copies = [remote(xv, nbuf.at[me_t], n_sems, (k - 1,), t_id(k)) for k in range(1, nt)]
    for c in copies + n_copies:
        c.start()
    pending += copies + n_copies
    place_row = place_row_ref[...]
    to_slots = flag(place_row == iota((batch, batch), 0))
    for c in copies:
        c.wait_recv()
    squares = sq_send[...]
    for k in range(ng - 1):
        squares = squares + sq_recv[k]
    fbuf[me_t] = lax.rsqrt(squares / total_feat + 1e-05)
    f_copies = [
        remote(fbuf.at[me_t], fbuf.at[me_t], f_sems, (k - 1,), t_id(k)) for k in range(1, nt)
    ]
    for c in f_copies:
        c.start()
    pending += f_copies
    small[1].wait()
    for c in n_copies + f_copies:
        c.wait_recv()
    o_copy.start()
    m_copies[0].start()
    for c in small[5:]:
        c.start()
    factors = fbuf[...].reshape(batch, LANES)[:, :1]
    normed = nbuf[...].astype(F32).reshape(batch, feat) * factors * gainv[...]
    normed = matmul(to_slots, normed.astype(BF16)).astype(BF16)

    cols = math.gcd(COLUMNS, width)

    def exchange_chips(j):
        for c in c_copies[j]:
            c.wait_recv()
        total = tbuf[j, me_c]
        for k in range(nc - 1):
            total = total + cbuf[k, j]
        sbuf[j] = total
        step = [
            remote(sbuf.at[j, r_peer(k)], rbuf.at[k - 1, j], t_sems, (k - 1, j), {"rows": r_peer(k)})
            for k in range(1, nr)
        ]
        for c in step:
            c.start()
        return step

    c_copies, t_copies = [], []
    for j in range(3):
        a_copies[j].wait()

        def attn_step(c, carry, j=j):
            at = slice(c * cols, (c + 1) * cols)
            term = matmul(normed, wa[j, :, at])
            for g in range(ng):
                tbuf[j, g % nc, g // nc, :, at] = term[g * slots : (g + 1) * slots]
            return carry

        for c in range(width // cols):
            attn_step(c, 0)
        if j < 2:
            m_copies[1 + j].start()
        step = [
            remote(tbuf.at[j, c_peer(k)], cbuf.at[k - 1, j], c_sems, (k - 1, j), {"role": c_peer(k)})
            for k in range(1, nc)
        ]
        for c in step:
            c.start()
        c_copies.append(step)
        pending += step
        if j > 0:
            t_copies.append(exchange_chips(j - 1))
    t_copies.append(exchange_chips(2))
    for step in t_copies:
        pending += step

    def projected(j):
        for c in t_copies[j]:
            c.wait_recv()
        total = sbuf[j, me_r]
        for k in range(nr - 1):
            total = total + rbuf[k, j]
        return total.astype(BF16)

    rows = slots * heads
    expand_mask = quotient(iota((rows, slots), 0), heads) == iota((rows, slots), 1)
    expand = flag(expand_mask)
    collapse = flag(quotient(iota((slots, rows), 1), heads) == iota((slots, rows), 0))
    row_at = iota((rows, width), 0)
    head_mask = quotient(iota((rows, width), 1), HEAD_DIM) == row_at - heads * quotient(row_at, heads)
    row_at = iota((rows, slots * ctx), 0)
    col_at = iota((rows, slots * ctx), 1)
    col_slot = quotient(col_at, ctx)
    row_length = jnp.sum(
        jnp.where(expand_mask, lens_ref[...].astype(F32), 0.0), axis=1, keepdims=True
    )
    live = (quotient(row_at, heads) == col_slot) & (
        (col_at - ctx * col_slot).astype(F32) < row_length
    )

    small[3].wait()
    small[4].wait()

    scale = 1.0 / math.sqrt(HEAD_DIM)
    spread = jnp.where(head_mask, matmul(expand, projected(0)), 0.0).astype(BF16)
    scores = matmul_nt(spread, kv[...].reshape(slots * ctx, width)) * scale
    own = (
        jnp.sum(
            jnp.where(expand_mask, matmul_nt(spread, projected(1)), 0.0), axis=1, keepdims=True
        )
        * scale
    )
    top = jnp.maximum(jnp.max(jnp.where(live, scores, -jnp.inf), axis=1, keepdims=True), own)
    probs = jnp.where(live, jnp.exp(scores - top), 0.0)
    self_prob = jnp.exp(own - top)
    total = jnp.sum(probs, axis=1, keepdims=True) + self_prob
    weights = (probs / total).astype(BF16)
    self_weight = (self_prob / total).astype(BF16).astype(F32)
    mixed = matmul(weights, vv[...].reshape(slots * ctx, width))
    mixed = mixed + self_weight * matmul(expand, projected(2))
    mixed = jnp.where(head_mask, mixed, 0.0).astype(BF16)
    hbuf[me_g] = matmul(collapse, mixed).astype(BF16)
    copies = [
        remote(hbuf.at[me_g], hbuf.at[me_g], h_sems, (k - 1,), g_id(k)) for k in range(1, ng)
    ]
    for c in copies:
        c.start()
    pending += copies
    o_copy.wait()
    for c in copies:
        c.wait_recv()
    heads_out = hbuf[...].astype(F32).reshape(batch, width).astype(BF16)
    heads_out = matmul_tn(to_slots, heads_out).astype(BF16)

    pieces, ocols = obuf.shape[0], obuf.shape[3]
    o_copies, a_out = [], []
    for p in range(pieces):
        term = matmul(heads_out, wo[:, p * ocols : (p + 1) * ocols])
        for t in range(nt):
            obuf[p, t] = term[t * xb : (t + 1) * xb].astype(BF16)
        step = [
            remote(obuf.at[p, t_peer(k)], robuf.at[p, k - 1], o_sems, (p, k - 1), t_id(k))
            for k in range(1, nt)
        ]
        for c in step:
            c.start()
        o_copies.append(step)
        pending += step
    for p in range(pieces):
        for c in o_copies[p]:
            c.wait_recv()
        head_sums = obuf[p, me_t].astype(F32)
        for k in range(nt - 1):
            head_sums = head_sums + robuf[p, k].astype(F32)
        at = slice(p * ocols, (p + 1) * ocols)
        attended = (xv[:, at].astype(F32) + head_sums).astype(BF16)
        att_ref[:, at] = attended
        abuf[p, me_t] = attended
        step = [
            remote(abuf.at[p, me_t], abuf.at[p, me_t], a_sems, (p, k - 1), t_id(k))
            for k in range(1, nt)
        ]
        for c in step:
            c.start()
        a_out.append(step)
        pending += step
    small[2].wait()

    gained, squares = [], 0.0
    for p in range(pieces):
        for c in a_out[p]:
            c.wait_recv()
        wide = abuf[p].astype(F32).reshape(batch, ocols)
        squares = squares + jnp.sum(wide * wide, axis=1, keepdims=True)
        gained.append((wide * mgainv[:, p * ocols : (p + 1) * ocols]).astype(BF16))
    gained = jnp.concatenate(gained, axis=1)
    for g in range(ng):
        msq_send[g] = jnp.broadcast_to(squares[g * slots : (g + 1) * slots], msq_send.shape[1:])
    msq_copies = [
        remote(msq_send.at[g_peer(k)], msq_recv.at[k - 1], msq_sems, (k - 1,), g_id(k))
        for k in range(1, ng)
    ]
    for c in msq_copies:
        c.start()
    pending += msq_copies

    m_steps = []
    for j in range(3):
        m_copies[j].wait()

        step = []
        for i in range(width // cols):
            at = slice(i * cols, (i + 1) * cols)
            weight = wm[:, at] if j == 0 else wa[j - 1, :, at]
            term = matmul(gained, weight)
            for g in range(ng):
                mbuf[j, i, g] = term[g * slots : (g + 1) * slots].astype(BF16)
            piece = [
                remote(
                    mbuf.at[j, i, g_peer(k)], rmbuf.at[j, i, k - 1], m_sems, (k - 1, j, i), g_id(k)
                )
                for k in range(1, ng)
            ]
            for c in piece:
                c.start()
            step.append(piece)
            pending += piece
        m_steps.append(step)

    for c in small[5:]:
        c.wait()
    for c in msq_copies:
        c.wait_recv()
    squares = msq_send[me_g]
    for k in range(ng - 1):
        squares = squares + msq_recv[k]
    scale_rows = lax.rsqrt(squares[:, :1] / total_feat + 1e-05)
    conv = []
    for j in range(3):
        total = []
        for i, piece in enumerate(m_steps[j]):
            for c in piece:
                c.wait_recv()
            part = mbuf[j, i, me_g].astype(F32)
            for k in range(ng - 1):
                part = part + rmbuf[j, i, k].astype(F32)
            total.append(part)
        total = jnp.concatenate(total, axis=1)
        conv.append(
            otv[0, j : j + 1] * (total * scale_rows)
            + otv[1, j : j + 1] * osv[0, j].astype(F32)
            + otv[2, j : j + 1] * osv[1, j].astype(F32)
        )
    product = conv[0] * conv[2]
    filtered = (
        itv[0:1] * product + itv[1:2] * isv[0].astype(F32) + itv[2:3] * isv[1].astype(F32)
    )
    gated_ref[...] = (conv[1] * filtered).astype(BF16)
    for c in pending:
        c.wait_send()


def local(
    nt,
    nr,
    nc,
    residual,
    attn_gain,
    attn_proj,
    cache_keys,
    cache_values,
    lengths,
    placement,
    out_proj,
    mix_gain,
    mix_proj,
    outer_taps,
    outer_state,
    inner_taps,
    inner_state,
):
    ng = nr * nc
    xb, feat = residual.shape
    slots = lengths.shape[0]
    batch = placement.shape[0]
    width = attn_proj.shape[2]
    anywhere = pl.BlockSpec(memory_space=pl.ANY)
    vmem = pl.BlockSpec(memory_space=pltpu.VMEM)
    dma = pltpu.SemaphoreType.DMA
    others_g, others_t = max(ng - 1, 1), max(nt - 1, 1)
    others_r, others_c = max(nr - 1, 1), max(nc - 1, 1)
    ocols, wcols = math.gcd(COLUMNS, feat), math.gcd(COLUMNS, width)
    pieces = feat // ocols
    weight_values = attn_proj.size + out_proj.size + mix_proj.size
    return pl.pallas_call(
        functools.partial(kernel, nt, nr, nc),
        out_shape=(
            jax.ShapeDtypeStruct((xb, feat), BF16),
            jax.ShapeDtypeStruct((slots, width), BF16),
        ),
        in_specs=[anywhere] * 5 + [vmem] * 2 + [anywhere] * 7,
        out_specs=(vmem, vmem),
        scratch_shapes=[
            pltpu.VMEM((xb, feat), BF16),
            pltpu.VMEM((1, feat), F32),
            pltpu.VMEM((1, feat), F32),
            pltpu.VMEM(attn_proj.shape, BF16),
            pltpu.VMEM(out_proj.shape, BF16),
            pltpu.VMEM(mix_proj.shape[1:], BF16),
            pltpu.VMEM(cache_keys.shape, BF16),
            pltpu.VMEM(cache_values.shape, BF16),
            pltpu.VMEM(outer_taps.shape, F32),
            pltpu.VMEM(outer_state.shape, BF16),
            pltpu.VMEM(inner_taps.shape, F32),
            pltpu.VMEM(inner_state.shape, BF16),
            pltpu.VMEM((xb, LANES), F32),
            pltpu.VMEM((others_g, xb, LANES), F32),
            pltpu.VMEM((nt, xb, feat), BF16),
            pltpu.VMEM((nt, xb, LANES), F32),
            pltpu.VMEM((3, nc, nr, slots, width), F32),
            pltpu.VMEM((others_c, 3, nr, slots, width), F32),
            pltpu.VMEM((3, nr, slots, width), F32),
            pltpu.VMEM((others_r, 3, slots, width), F32),
            pltpu.VMEM((ng, slots, width), BF16),
            pltpu.VMEM((pieces, nt, xb, ocols), BF16),
            pltpu.VMEM((pieces, others_t, xb, ocols), BF16),
            pltpu.VMEM((pieces, nt, xb, ocols), BF16),
            pltpu.VMEM((ng, slots, LANES), F32),
            pltpu.VMEM((others_g, slots, LANES), F32),
            pltpu.VMEM((3, width // wcols, ng, slots, wcols), BF16),
            pltpu.VMEM((3, width // wcols, others_g, slots, wcols), BF16),
            dma((9,)),
            dma((7,)),
            dma((2, others_g)),
            dma((2, others_t)),
            dma((2, others_t)),
            dma((2, others_c, 3)),
            dma((2, others_r, 3)),
            dma((2, others_g)),
            dma((2, pieces, others_t)),
            dma((2, pieces, others_t)),
            dma((2, others_g)),
            dma((2, others_g, 3, width // wcols)),
        ],
        compiler_params=pltpu.CompilerParams(
            collective_id=0, has_side_effects=True, vmem_limit_bytes=58 * 2**20
        ),
        cost_estimate=pl.CostEstimate(
            flops=2 * batch * weight_values, bytes_accessed=2 * weight_values, transcendentals=0
        ),
        name="hybrid_block",
    )(
        residual,
        attn_gain.reshape(1, feat),
        attn_proj,
        cache_keys,
        cache_values,
        lengths.reshape(1, slots),
        placement.reshape(1, batch),
        out_proj,
        mix_gain.reshape(1, feat),
        mix_proj,
        outer_taps,
        outer_state,
        inner_taps,
        inner_state,
    )


def solution(mesh):
    return jax.shard_map(
        functools.partial(local, mesh.shape["tensor"], mesh.shape["rows"], mesh.shape["role"]),
        mesh=mesh,
        in_specs=(
            P(("groups", "tensor"), ("rows", "role")),
            P(("rows", "role")),
            P(None, ("rows", "role"), "tensor"),
            P(("groups", "rows", "role"), None, "tensor"),
            P(("groups", "rows", "role"), None, "tensor"),
            P(("groups", "rows", "role")),
            P("groups"),
            P("tensor", ("rows", "role")),
            P(("rows", "role")),
            P(None, ("rows", "role"), "tensor"),
            P(None, None, "tensor"),
            P(None, None, ("groups", "rows", "role"), "tensor"),
            P(None, "tensor"),
            P(None, ("groups", "rows", "role"), "tensor"),
        ),
        out_specs=(
            P(("groups", "tensor"), ("rows", "role")),
            P(("groups", "rows", "role"), "tensor"),
        ),
        check_vma=False,
    )
```
